32 devices in a mesh: dp: 4 (over x, core), expert: 8 (over z, y).
Axes of the slice: x: 2, y: 2, z: 4, core: 2. Of those that a mesh axis runs over, the one named last changes fastest.
Arguments:
- activations: bfloat16 [4096, 2048], P(('dp', 'expert')), may hold values from -6 to 6
- routed_experts: int32 [4096, 2], P(('dp', 'expert')), may hold values from 0 to 7, all different within a row; in each aligned block of 128 rows (0 to 127, 128 to 255, ...) at most 32 rows name the same one
- route_weights: float32 [4096, 2], P(('dp', 'expert')), may hold values from 0.25 to 1
- live_counts: int32 [4, 8], P('dp', 'expert'), may hold values from 32 to 128, as said below
- swap_partner: int32 [8], replicated, may hold values from 0 to 7, as said below
- gate_proj: bfloat16 [8, 2048, 768], P('expert', 'dp'), may hold values from -0.125 to 0.125
- up_proj: bfloat16 [8, 2048, 768], P('expert', 'dp'), may hold values from -0.125 to 0.125
- down_proj: bfloat16 [8, 2048, 768], P('expert', 'dp'), may hold values from -0.21875 to 0.21875
- first_moment: bfloat16 [8, 2048, 768], P('expert', 'dp'), may hold values from -6 to 6
- second_moment: bfloat16 [8, 2048], P('expert', 'dp'), may hold values from 0.5 to 20
Outputs:
- layer_output: bfloat16 [4096, 2048], P(('dp', 'expert'))
- update_direction: bfloat16 [8, 2048, 768], P('expert', 'dp')
The draws below stay inside these ranges and needn't reach their ends.
Inputs may be any that keep to these rules, and one draw needn't show every extreme that they name: `routed_experts`: each token names 2 different experts; the 256 routed rows of one device name every expert exactly 32 times. The first live_counts tokens of a device's block are live, the rest are padding; some device has all 128 live. swap_partner[i] = i XOR p, where p is 4 or 2, the same for all i, so devices are swapped in pairs; expert i moves to device swap_partner[i].
All inputs are finite; a program needn't handle non-finite values.
Results may differ from the reference program's by a relative error of at most 0.015.
Values may be sent and summed in bfloat16 or wider, within the bound.
No kernel may reach another device: no remote copies, remote signals or barrier semaphores. Data moves between devices by JAX's collectives and lax.ppermute only.
A program may use at most 64 MiB of HBM per device.

```python
import math
import jax
import jax.numpy as jnp
import numpy as np
from jax import lax

D = 2048
FW = 768
TOPF = 2
TOK_DEV = 128
EXPERTS = 8
CAP = 32
TOKENS = 4096
N_DP = 4
N_EXPERT = 8


def draw_swap_partner(key, part):
    levels = EXPERTS.bit_length() - 1
    bit_place = jax.random.randint(key, (), levels - 2, levels)
    power = jnp.left_shift(jnp.int32(1), bit_place.astype(jnp.int32))
    return jnp.bitwise_xor(jnp.arange(EXPERTS, dtype=jnp.int32), power).astype(jnp.int32)


def draw_live_counts(key, part):
    lowest = max(TOK_DEV // 4, 1)
    drawn = jax.random.randint(key, (N_DP * N_EXPERT,), lowest, TOK_DEV + 1)
    chosen = jax.random.randint(jax.random.fold_in(key, 7), (), 0, N_DP * N_EXPERT)
    flattened = jnp.where(jnp.arange(N_DP * N_EXPERT) == chosen, TOK_DEV, drawn)
    return flattened.reshape(N_DP, N_EXPERT).astype(jnp.int32)


def block_levels(key, extent, split, least, high):
    gain, own = 1.0, jax.random.fold_in(key, 6)
    for dim, shards_of in split:
        heights = jnp.exp(jax.random.uniform(jax.random.fold_in(own, dim), (shards_of,), jnp.float32, least / len(split), high / len(split)))
        gain = gain * jnp.repeat(heights, extent[dim] // shards_of).reshape([-1 if axis == dim else 1 for axis in range(len(extent))])
    return gain


def shared_out(stream_key, own, number, rows, amount, top, limit, skew):
    ranking = jax.random.permutation(stream_key, amount)
    heavy_load, ordinary = shares(amount, rows * top, limit, skew, True), shares(amount, rows * top, limit, skew, False)
    places = jnp.arange(amount)

    def named(sizes, turn):
        used = int((sizes > 0).sum())
        fixed = max(1, used // 4)
        shifted = fixed + (places - fixed + turn * (used - fixed)) % max(1, amount - fixed)
        return jnp.zeros((amount,), jnp.int32).at[ranking[jnp.where(places < fixed, places, shifted)]].set(jnp.asarray(sizes, jnp.int32))

    sizes = jnp.where(number % 4 == 0, named(heavy_load, number // 4), named(ordinary, number - number // 4 - 1))
    mixed = jax.random.permutation(jax.random.fold_in(own, 3), amount)
    donor, taker = mixed[0:amount // 2 * 2:2], mixed[1:amount // 2 * 2:2]
    slack = jnp.minimum(sizes[donor] - 1, limit - sizes[taker]) // 2
    slack = jnp.where((donor == ranking[0]) | (taker == ranking[0]) | (sizes[taker] == 0), 0, jnp.maximum(slack, 0))
    shifted = jax.random.randint(jax.random.fold_in(own, 4), (amount // 2,), 0, 1 << 20) % (slack + 1)
    sizes = sizes.at[donor].add(-shifted).at[taker].add(shifted)
    members = jnp.searchsorted(jnp.cumsum(sizes), jnp.arange(rows * top), side="right").astype(jnp.int32)
    table = members.reshape(top, rows).T
    table = table[jax.random.permutation(jax.random.fold_in(own, 1), rows)]
    turn = jax.random.randint(jax.random.fold_in(own, 2), (rows, 1), 0, top)
    return jnp.take_along_axis(table, (jnp.arange(top)[None, :] + turn) % top, axis=1)


def shares(number_of, total, most, slope, full):
    weights = [(1 << 20) // math.isqrt(standing ** slope) + 1 for standing in range(1, number_of + 1)]
    largest = most if full else min(most, max(-(-total // number_of), total * weights[0] // sum(weights)))
    least = 1 if total - largest >= number_of - 1 else 0
    counts, rest = [largest] + [least] * (number_of - 1), total - largest - least * (number_of - 1)
    while rest > 0:
        movable = [i for i in range(1, number_of) if counts[i] < largest] or [i for i in range(1, number_of) if counts[i] < most]
        mass, budget = sum([weights[i] for i in movable]), rest
        for i in movable:
            more = min(most - counts[i], max(1, budget * weights[i] // mass), rest)
            counts[i] = counts[i] + more
            rest = rest - more
    return np.array(counts)


def bell_draw(rng, extent, width, bound, split=(), held_as=jnp.bfloat16):
    values = width * jax.random.normal(rng, extent, jnp.float32)
    if split:
        values = values * block_levels(rng, extent, split, -0.22, 0.18)
    return jnp.clip(values, -bound, bound).astype(held_as)


def setup_inputs(seed: int = 0) -> dict:
    arg_keys = jax.random.split(jax.random.key(seed), 11)
    activations = bell_draw(arg_keys[0], (TOKENS, D), 1.0, 6.0, ((0, 32),))
    routed_experts_keys = jax.random.split(jax.random.fold_in(arg_keys[1], 1), TOKENS // TOK_DEV)
    routed_experts_turns = jax.random.permutation(jax.random.fold_in(arg_keys[1], 3), TOKENS // TOK_DEV)
    routed_experts = jax.vmap(lambda own, number: shared_out(jax.random.fold_in(arg_keys[1], 2), own, number, TOK_DEV, EXPERTS, TOPF, CAP, 0))(routed_experts_keys, routed_experts_turns).reshape((TOKENS, TOPF))
    route_weights = jnp.clip(0.25 + 0.75 * jax.random.uniform(arg_keys[2], (TOKENS, TOPF), jnp.float32) ** block_levels(arg_keys[2], (TOKENS, TOPF), ((0, 32),), -0.2, 0.2), 0.25, 1.0)
    live_counts = draw_live_counts(jax.random.fold_in(arg_keys[10], 71), 0)
    swap_partner = draw_swap_partner(jax.random.fold_in(arg_keys[10], 71), 0)
    gate_proj = bell_draw(arg_keys[5], (EXPERTS, D, FW), D ** -0.5, 0.125, ((0, 8), (1, 4)))
    up_proj = bell_draw(arg_keys[6], (EXPERTS, D, FW), D ** -0.5, 0.125, ((0, 8), (1, 4)))
    down_proj = bell_draw(arg_keys[7], (EXPERTS, D, FW), FW ** -0.5, 0.21875, ((0, 8), (1, 4)))
    first_moment = bell_draw(arg_keys[8], (EXPERTS, D, FW), 1.0, 6.0, ((0, 8), (1, 4)))
    second_moment = jnp.clip(jnp.exp(math.log(20.0) - 3.6888795 * jax.random.uniform(arg_keys[9], (EXPERTS, D), jnp.float32) ** block_levels(arg_keys[9], (EXPERTS, D), ((0, 8), (1, 4)), -0.2, 0.2)), 0.5, 20.0).astype(jnp.bfloat16)
    return {"activations": activations, "routed_experts": routed_experts, "route_weights": route_weights, "live_counts": live_counts, "swap_partner": swap_partner, "gate_proj": gate_proj, "up_proj": up_proj, "down_proj": down_proj, "first_moment": first_moment, "second_moment": second_moment}


def reference(activations, routed_experts, route_weights, live_counts, swap_partner, gate_proj, up_proj, down_proj, first_moment, second_moment):
    devices = N_DP * N_EXPERT
    routed = TOK_DEV * TOPF
    expert_ids = routed_experts.reshape(devices, routed)
    columns = jnp.arange(EXPERTS, dtype=jnp.int32)
    matches = (expert_ids[:, :, None] == columns[None, None, :]).astype(jnp.int32)
    rank_table = lax.optimization_barrier(jnp.sum(matches * (jnp.cumsum(matches, axis=1) - 1), axis=2)).astype(jnp.int32)
    device_index = jnp.broadcast_to(jnp.arange(devices, dtype=jnp.int32)[:, None], (devices, routed))
    row_index = jnp.broadcast_to(jnp.arange(routed, dtype=jnp.int32)[None, :], (devices, routed))
    placed = jnp.zeros((EXPERTS, devices, CAP), jnp.int32).at[expert_ids, device_index, rank_table].set(row_index)
    token_rows = activations.reshape(devices, TOK_DEV, D)
    device_column = jnp.arange(devices, dtype=jnp.int32)[:, None]

    def forward_expert(operands):
        placement_rows, gate_w, up_w, down_w = operands
        chosen = token_rows[device_column, placement_rows // TOPF].reshape(devices * CAP, D)
        gate_sum = jnp.dot(chosen, gate_w, preferred_element_type=jnp.float32)
        up_sum = jnp.dot(chosen, up_w, preferred_element_type=jnp.float32)
        hidden = (jax.nn.silu(gate_sum) * up_sum).astype(jnp.bfloat16)
        produced = jnp.dot(hidden, down_w.T, preferred_element_type=jnp.float32).astype(jnp.bfloat16)
        return (produced.reshape(devices, CAP, D), hidden.reshape(devices, CAP, FW))
    produced_all, hidden_all = lax.map(forward_expert, (placed, gate_proj, up_proj, down_proj))
    gathered = produced_all[expert_ids, device_index, rank_table].reshape(devices, TOK_DEV, TOPF, D)
    weights = route_weights.reshape(devices, TOK_DEV, TOPF)
    total = jnp.zeros((devices, TOK_DEV, D), jnp.float32)
    for choice_index in range(TOPF):
        total = total + gathered[:, :, choice_index].astype(jnp.float32) * weights[:, :, choice_index, None]
    live_mask = (jnp.arange(TOK_DEV, dtype=jnp.int32)[None, :] < live_counts.reshape(devices)[:, None]).astype(jnp.float32)
    layer_output = (total * live_mask[:, :, None]).astype(jnp.bfloat16)
    cotangent = (weights[:, :, :, None] * layer_output.astype(jnp.float32)[:, :, None, :]).astype(jnp.bfloat16)
    cotangent = cotangent.reshape(devices, routed, D)

    def update_expert(operands):
        placement_rows, hidden, first_state, second_state = operands
        picked = cotangent[device_column, placement_rows].reshape(N_DP, N_EXPERT * CAP, D).astype(jnp.float32)
        hidden_group = hidden.reshape(N_DP, N_EXPERT * CAP, FW).astype(jnp.float32)
        partial_sums = jnp.einsum('qrd,qrf->qdf', picked, hidden_group).astype(jnp.bfloat16)
        gradient = lax.optimization_barrier(jnp.sum(partial_sums.astype(jnp.float32), axis=0))
        first_new = 0.9 * first_state.astype(jnp.float32) + 0.1 * gradient
        second_new = 0.99 * second_state.astype(jnp.float32) + 0.01 * lax.optimization_barrier(jnp.mean(gradient * gradient, axis=1))
        return (first_new / (jnp.sqrt(second_new)[:, None] + 1e-08)).astype(jnp.bfloat16)
    steps_all = lax.map(update_expert, (placed, hidden_all, first_moment, second_moment))
    update_direction = steps_all[swap_partner]
    return (layer_output.reshape(TOKENS, D), update_direction)
```

```python
from functools import partial

import jax
import jax.numpy as jnp
from jax import lax
from jax.sharding import PartitionSpec as P

BF = jnp.bfloat16
F32 = jnp.float32


def trade(block, axis, offset):
    count = lax.axis_size(axis)
    return lax.ppermute(block, axis, [(i, i ^ offset) for i in range(count)])


def by_offset(blocks, place):
    a, b, c, d = blocks
    odd = (place & 1) == 1
    a, b, c, d = (
        jnp.where(odd, b, a),
        jnp.where(odd, a, b),
        jnp.where(odd, d, c),
        jnp.where(odd, c, d),
    )
    far = (place & 2) == 2
    return [
        jnp.where(far, c, a),
        jnp.where(far, d, b),
        jnp.where(far, a, c),
        jnp.where(far, b, d),
    ]


def slots_of(table, capacity):
    tokens = table.shape[1]
    chosen = table != 0
    before = (jnp.arange(tokens)[:, None] < jnp.arange(tokens)[None, :]).astype(BF)
    rank = jnp.dot(chosen.astype(BF), before, preferred_element_type=F32)
    place = jnp.arange(capacity, dtype=F32)
    return chosen[:, None, :] & (rank[:, None, :] == place[None, :, None])


def exchange(rows):
    return lax.all_to_all(rows, "expert", split_axis=0, concat_axis=0, tiled=True)


def combine(returned, tables, slots):
    out = []
    for g in range(2):
        weight = jnp.where(slots[g], jnp.maximum(tables[g], 0.0)[:, None, :], 0.0)
        high = weight.astype(BF)
        low = (weight - high.astype(F32)).astype(BF)
        rows = returned[:, g]
        total = jnp.einsum("ect,ecf->tf", high, rows, preferred_element_type=F32)
        total = total + jnp.einsum("ect,ecf->tf", low, rows, preferred_element_type=F32)
        out.append(total.astype(BF))
    return out


def cotangents(outs, tables, slots, offset):
    experts = tables[0].shape[0]
    placed = jnp.arange(experts) ^ offset
    sending = []
    for g in range(2):
        weight = jnp.sum(jnp.where(slots[g], jnp.abs(tables[g])[:, None, :], 0.0), axis=2)
        picked = jnp.einsum("ect,tf->ecf", slots[g].astype(BF), outs[g], preferred_element_type=F32)
        sending.append((picked * weight[:, :, None]).astype(BF))
    both = jnp.stack(sending, axis=1)
    shape = both.shape
    both = both.reshape((experts // (2 * offset), 2, offset) + shape[1:])[:, ::-1]
    return both.reshape(shape)


def work(operands, shift_bit):
    (
        activations,
        routed_experts,
        route_weights,
        live_counts,
        gate_proj,
        up_proj,
        down_proj,
        first_moment,
        second_moment,
    ) = operands
    offset = 1 << shift_bit
    experts = lax.axis_size("expert")
    place = lax.axis_index("dp")
    tokens, choices = routed_experts.shape
    capacity = tokens * choices // experts
    width = activations.shape[1]
    block = gate_proj.shape[1]
    hidden_width = gate_proj.shape[2]

    ids, weights = routed_experts.T, route_weights.T
    names = jnp.arange(experts, dtype=jnp.int32)[:, None]
    table = jnp.zeros((experts, tokens), F32)
    for k in range(choices):
        table = table + jnp.where(ids[k][None, :] == names, weights[k][None, :], 0.0)
    live = jnp.arange(tokens, dtype=jnp.int32)[None, :] < live_counts[0, 0]
    table = jnp.where(live, table, -table)

    slots0 = slots_of(table, capacity)
    ordered = jnp.concatenate(
        by_offset([activations[:, i * block : (i + 1) * block] for i in range(4)], place), axis=1
    )
    outgoing = jnp.einsum("ect,tf->ecf", slots0.astype(BF), ordered, preferred_element_type=F32)
    outgoing = outgoing.astype(BF)

    gate, up = gate_proj[0], up_proj[0]
    gate2, up2 = trade(gate, "dp", 2), trade(up, "dp", 2)
    arrived = exchange(outgoing).reshape(experts * capacity, width)
    gate1, up1 = trade(gate, "dp", 1), trade(up, "dp", 1)
    table2 = trade(table, "dp", 2)
    near_tables = trade(jnp.stack([table, table2]), "dp", 1)
    tables = [table, near_tables[0], table2, near_tables[1]]
    slots = [slots0] + [slots_of(t, capacity) for t in tables[1:]]

    first_in, arrived = lax.optimization_barrier((first_moment, arrived))
    first = trade(first_in, "expert", offset)
    second = trade(second_moment, "expert", offset)

    gate3, up3 = trade(gate2, "dp", 1), trade(up2, "dp", 1)
    columns = [arrived[:, i * block : (i + 1) * block] for i in range(4)]
    gate_sum = sum(
        jnp.dot(c, w, preferred_element_type=F32) for c, w in zip(columns, (gate, gate1, gate2, gate3))
    )
    up_sum = sum(
        jnp.dot(c, w, preferred_element_type=F32) for c, w in zip(columns, (up, up1, up2, up3))
    )
    hidden = (jax.nn.silu(gate_sum) * up_sum).astype(BF).reshape(experts, capacity, hidden_width)

    def pair(a, b):
        return jnp.stack([a, b], axis=1)

    def produce(rows):
        made = jnp.einsum("egcf,nf->egcn", rows, down_proj[0], preferred_element_type=F32)
        return made.astype(BF)

    hidden1 = trade(hidden, "dp", 1)
    hidden2 = trade(hidden, "dp", 2)
    moved = trade(hidden, "expert", offset)
    back_near = exchange(produce(pair(hidden, hidden1)))
    hidden3 = trade(hidden2, "dp", 1)
    back_far = exchange(produce(pair(hidden2, hidden3)))

    moved1 = trade(moved, "dp", 1)
    moved2 = trade(moved, "dp", 2)
    moved3 = trade(moved2, "dp", 1)

    out_near = combine(back_near, tables[:2], slots[:2])
    cot_near = exchange(cotangents(out_near, tables[:2], slots[:2], offset))
    out_far = combine(back_far, tables[2:], slots[2:])
    cot_far = exchange(cotangents(out_far, tables[2:], slots[2:], offset))

    mine = [out_near[0]] + [
        trade(o, "dp", i + 1) for i, o in enumerate((out_near[1], out_far[0], out_far[1]))
    ]
    layer_output = jnp.concatenate(by_offset(mine, place), axis=1)

    gradient = jnp.einsum("egcn,egcf->nf", cot_near, pair(moved, moved1), preferred_element_type=F32)
    gradient = gradient + jnp.einsum(
        "egcn,egcf->nf", cot_far, pair(moved2, moved3), preferred_element_type=F32
    )
    first_new = 0.9 * first[0].astype(F32) + 0.1 * gradient
    second_new = 0.99 * second[0].astype(F32) + 0.01 * jnp.mean(gradient * gradient, axis=1)
    step = (first_new / (jnp.sqrt(second_new)[:, None] + 1e-08)).astype(BF)
    return layer_output, step[None]


def local(
    activations,
    routed_experts,
    route_weights,
    live_counts,
    swap_partner,
    gate_proj,
    up_proj,
    down_proj,
    first_moment,
    second_moment,
):
    levels = swap_partner.shape[0].bit_length() - 1
    operands = (
        activations,
        routed_experts,
        route_weights,
        live_counts,
        gate_proj,
        up_proj,
        down_proj,
        first_moment,
        second_moment,
    )
    branches = [partial(work, shift_bit=bit) for bit in (levels - 2, levels - 1)]
    return lax.cond(swap_partner[0] == 1 << (levels - 1), branches[1], branches[0], operands)


def solution(mesh):
    in_specs = (
        P(("dp", "expert"), None),
        P(("dp", "expert"), None),
        P(("dp", "expert"), None),
        P("dp", "expert"),
        P(),
        P("expert", "dp", None),
        P("expert", "dp", None),
        P("expert", "dp", None),
        P("expert", "dp", None),
        P("expert", "dp"),
    )
    out_specs = (P(("dp", "expert"), None), P("expert", "dp", None))
    return jax.shard_map(local, mesh=mesh, in_specs=in_specs, out_specs=out_specs, check_vma=False)
```

```python
from functools import partial

import jax
import jax.numpy as jnp
from jax import lax
from jax.experimental import pallas as pl
from jax.experimental.pallas import tpu as pltpu
from jax.sharding import PartitionSpec as P

BF = jnp.bfloat16
F32 = jnp.float32
after = lax.optimization_barrier


def trade(block, axis, offset):
    count = lax.axis_size(axis)
    return lax.ppermute(block, axis, [(i, i ^ offset) for i in range(count)])


def by_offset(blocks, place):
    blocks = list(blocks)
    bit = 1
    while bit < len(blocks):
        on = (place & bit) == bit
        blocks = [jnp.where(on, blocks[i ^ bit], blocks[i]) for i in range(len(blocks))]
        bit *= 2
    return blocks


def rows_at(table, offset):
    parts = table.reshape(-1, 2, offset, table.shape[1])
    return jnp.concatenate([parts[:, 1:], parts[:, :1]], axis=1).reshape(table.shape)


def call(kernel, out_shape, *operands, **options):
    return pl.pallas_call(
        kernel,
        out_shape=out_shape,
        compiler_params=pltpu.CompilerParams(vmem_limit_bytes=16 << 20),
        **options,
    )(*operands)


def dot(a, b):
    return jnp.dot(a, b, preferred_element_type=F32)


def dot_columns(a, b):
    return lax.dot_general(a, b, (((1,), (1,)), ((), ())), preferred_element_type=F32)


def dot_rows(a, b):
    return lax.dot_general(a, b, (((0,), (0,)), ((), ())), preferred_element_type=F32)


def spread(table, capacity):
    experts, tokens = table.shape
    slots = experts * capacity
    chosen = table != 0
    earlier = lax.broadcasted_iota(jnp.int32, (tokens, tokens), 0)
    later = lax.broadcasted_iota(jnp.int32, (tokens, tokens), 1)
    rank = dot(jnp.where(chosen, 1.0, 0.0).astype(BF), jnp.where(earlier < later, 1.0, 0.0).astype(BF))
    rank = jnp.where(chosen, rank, -1.0).astype(BF)
    slot = lax.broadcasted_iota(jnp.int32, (slots, experts), 0)
    name = lax.broadcasted_iota(jnp.int32, (slots, experts), 1)
    owner = jnp.where(slot // capacity == name, 1.0, 0.0).astype(BF)
    place = (lax.broadcasted_iota(jnp.int32, (slots, tokens), 0) % capacity).astype(F32)
    return dot(owner, rank) == place, owner


def two_parts(value):
    high = value.astype(BF)
    return high, (value - high.astype(F32)).astype(BF)


def dispatch_kernel(place_ref, live_ref, ids_ref, weights_ref, act_ref, rows_ref, table_ref, *, capacity):
    experts, tokens = table_ref.shape
    lanes = max(experts, 128)
    name = lax.broadcasted_iota(jnp.int32, (tokens, lanes), 1)
    table = jnp.zeros((tokens, lanes), F32)
    for k in range(ids_ref.shape[1]):
        table = table + jnp.where(ids_ref[:, k : k + 1] == name, weights_ref[:, k : k + 1], 0.0)
    token = lax.broadcasted_iota(jnp.int32, (tokens, lanes), 0)
    table = jnp.where(token < live_ref[0, 0], table, -table)
    table = table.T[:experts]
    table_ref[...] = table
    chosen = jnp.where(spread(table, capacity)[0], 1.0, 0.0).astype(BF)
    block = act_ref.shape[1] // 4
    for i in range(4):
        source = pl.multiple_of((place_ref[0] ^ i) * block, block)
        rows_ref[:, i * block : (i + 1) * block] = dot(chosen, act_ref[:, pl.ds(source, block)]).astype(BF)


def gate_kernel(rows_ref, g0, g1, g2, g3, u0, u1, gate_ref, up_ref):
    block = g0.shape[0]
    columns = [rows_ref[:, i * block : (i + 1) * block] for i in range(4)]
    gate = sum(dot(c, w[...]) for c, w in zip(columns, (g0, g1, g2, g3)))
    gate_ref[...] = gate / (1.0 + jnp.exp(-gate))
    up_ref[...] = sum(dot(c, w[...]) for c, w in zip(columns, (u0, u1)))


def hidden_kernel(rows_ref, u2, u3, gate_ref, up_ref, hidden_ref):
    block = u2.shape[0]
    up = up_ref[...] + dot(rows_ref[:, :block], u2[...]) + dot(rows_ref[:, block:], u3[...])
    hidden_ref[...] = (gate_ref[...] * up).astype(BF)


def produce_kernel(*refs):
    *hidden, down_ref, out_ref = refs
    block = down_ref.shape[0]
    for g, ref in enumerate(hidden):
        out_ref[:, g * block : (g + 1) * block] = dot_columns(ref[...], down_ref[...]).astype(BF)


def maps_kernel(tables_ref, placed_ref, back_ref, sent_ref, weight_ref, *, capacity):
    for g in range(tables_ref.shape[0]):
        table = tables_ref[g]
        chosen, owner = spread(table, capacity)
        for i, part in enumerate(two_parts(jnp.maximum(table, 0.0))):
            back_ref[g, i] = jnp.where(chosen, dot(owner, part), 0.0).T.astype(BF)
        table = placed_ref[g]
        chosen, owner = spread(table, capacity)
        sent_ref[g] = jnp.where(chosen, 1.0, 0.0).astype(BF)
        high, low = two_parts(jnp.abs(table))
        weight = dot(owner, high) + dot(owner, low)
        weight_ref[g] = jnp.sum(jnp.where(chosen, weight, 0.0), axis=1, keepdims=True)


def combine_kernel(rows_ref, back_ref, sent_ref, weight_ref, o0, o1, o2, o3, cot_ref):
    for g, out_ref in enumerate((o0, o1, o2, o3)):
        columns = slice(g * out_ref.shape[1], (g + 1) * out_ref.shape[1])
        rows = rows_ref[:, columns]
        out = (dot(back_ref[g, 0], rows) + dot(back_ref[g, 1], rows)).astype(BF)
        out_ref[...] = out
        cot_ref[:, columns] = (dot(sent_ref[g], out) * weight_ref[g]).astype(BF)


def step_kernel(cot_ref, h0, h1, h2, h3, *refs, shares):
    *firsts, second_ref, out_ref = refs
    step = pl.program_id(0)
    part, block = out_ref.shape[0], cot_ref.shape[1] // 4
    first = firsts[-1][...]
    for i in range(len(firsts) - 2, -1, -1):
        first = jnp.where(step < sum(shares[: i + 1]), firsts[i][...], first)
    first = first.astype(F32)
    gradient = 0.0
    for g, hidden in enumerate((h0, h1, h2, h3)):
        start = pl.multiple_of(g * block + step * part, part)
        gradient = gradient + dot_rows(cot_ref[:, pl.ds(start, part)], hidden[...])
    first_new = 0.9 * first + 0.1 * gradient
    mean = jnp.sum(gradient * gradient, axis=1, keepdims=True) * (1.0 / gradient.shape[1])
    second_new = 0.99 * second_ref[...].astype(F32) + 0.01 * mean
    out_ref[...] = (first_new / (jnp.sqrt(second_new) + 1e-08)).astype(BF)


def shape(*dims, dtype=BF):
    return jax.ShapeDtypeStruct(dims, dtype)


SCALARS = pl.BlockSpec(memory_space=pltpu.SMEM)
WHOLE = pl.BlockSpec(memory_space=pltpu.VMEM)


def work(operands, shift_bit):
    (
        activations,
        routed_experts,
        route_weights,
        live_counts,
        gate_proj,
        up_proj,
        down_proj,
        first_moment,
        second_moment,
    ) = operands
    offset = 1 << shift_bit
    experts = lax.axis_size("expert")
    place = lax.axis_index("dp")
    tokens, choices = routed_experts.shape
    routed = tokens * choices
    capacity = routed // experts
    width = activations.shape[1]
    block, units = gate_proj.shape[1:]

    def exchange(rows):
        cut = rows.reshape(experts, capacity, rows.shape[1])
        return lax.all_to_all(cut, "expert", split_axis=0, concat_axis=0, tiled=True).reshape(rows.shape)

    gate, up, down = gate_proj[0], up_proj[0], down_proj[0]
    gate2 = trade(gate, "dp", 2)
    up_late, gate2 = after((up, gate2))
    up2 = trade(up_late, "dp", 2)
    gate1, up1 = trade(gate, "dp", 1), trade(up, "dp", 1)

    outgoing, table = call(
        partial(dispatch_kernel, capacity=capacity),
        (shape(routed, width), shape(experts, tokens, dtype=F32)),
        jnp.stack([place]).astype(jnp.int32),
        live_counts,
        routed_experts,
        route_weights,
        activations,
        in_specs=[SCALARS, SCALARS, WHOLE, WHOLE, WHOLE],
    )
    shares = (2, 1, 1) if shift_bit == experts.bit_length() - 3 else (1, 1, 2)
    quarter = block // 4
    ends = [sum(shares[:i]) * quarter for i in range(4)]

    def moment(source, i):
        return trade(source[0, ends[i] : ends[i + 1]], "expert", offset) if shares[i] else None

    first_a = moment(first_moment, 0)
    outgoing, first_a = after((outgoing, first_a))
    arrived = exchange(outgoing)
    first_late, second_late, _ = after((first_moment, second_moment, arrived))
    first_b = moment(first_late, 1)

    gate3 = trade(gate2, "dp", 1)
    column = pl.BlockSpec((block, 256), lambda i: (0, i))
    result = pl.BlockSpec((routed, 256), lambda i: (0, i))
    gate_sum, up_sum = call(
        gate_kernel,
        (shape(routed, units, dtype=F32),) * 2,
        arrived,
        gate,
        gate1,
        gate2,
        gate3,
        up,
        up1,
        grid=(units // 256,),
        in_specs=[pl.BlockSpec((routed, width), lambda i: (0, 0))] + [column] * 6,
        out_specs=(result, result),
    )
    up3 = trade(up2, "dp", 1)
    up_sum, first_b = after((up_sum, first_b))
    hidden = call(
        hidden_kernel,
        shape(routed, units),
        arrived,
        up2,
        up3,
        gate_sum,
        up_sum,
        grid=(units // 256,),
        in_specs=[pl.BlockSpec((routed, 2 * block), lambda i: (0, 1)), column, column, result, result],
        out_specs=result,
    )
    hidden2 = trade(hidden, "dp", 2)
    moved = trade(hidden, "expert", offset)
    hidden1 = trade(hidden, "dp", 1)
    hidden2, moved = after((hidden2, moved))
    hidden3 = trade(hidden2, "dp", 1)
    first_c = moment(first_late, 2)
    hidden3, first_c = after((hidden3, first_c))
    made = call(produce_kernel, shape(routed, 4 * block), hidden, hidden1, hidden2, hidden3, down)
    back = exchange(made)

    table_late, second_late, _ = after((table, second_late, hidden2))
    second = trade(second_late, "expert", offset)
    table2 = trade(table_late, "dp", 2)
    table1, table3 = trade(jnp.stack([table, table2]), "dp", 1)
    tables = [table, table1, table2, table3]
    back_map, sent_map, sent_weight = call(
        partial(maps_kernel, capacity=capacity),
        (shape(4, 2, tokens, routed), shape(4, routed, tokens), shape(4, routed, 1, dtype=F32)),
        jnp.stack(tables),
        jnp.stack([rows_at(t, offset) for t in tables]),
    )
    moved, _ = after((moved, back))
    moved2 = trade(moved, "dp", 2)
    moved1 = trade(moved, "dp", 1)
    moved3 = trade(moved2, "dp", 1)

    out0, out1, out2, out3, cot = call(
        combine_kernel,
        [shape(tokens, block)] * 4 + [shape(routed, 4 * block)],
        back,
        back_map,
        sent_map,
        sent_weight,
    )
    cot = exchange(cot)

    mine = [out0, trade(out1, "dp", 1), trade(out2, "dp", 2), trade(out3, "dp", 3)]
    layer_output = jnp.concatenate(by_offset(mine, place), axis=1)

    part = quarter
    step = call(
        partial(step_kernel, shares=[n for n in shares if n]),
        shape(block, units),
        cot,
        moved,
        moved1,
        moved2,
        moved3,
        *[f for f in (first_a, first_b, first_c) if f is not None],
        second.reshape(block, 1),
        grid=(block // part,),
        in_specs=[pl.BlockSpec((routed, 4 * block), lambda i: (0, 0))]
        + [pl.BlockSpec((routed, units), lambda i: (0, 0))] * 4
        + [
            pl.BlockSpec((part, units), lambda i, k=k, n=n: (jnp.clip(i - sum(shares[:k]), 0, n - 1), 0))
            for k, n in enumerate(shares)
            if n
        ]
        + [pl.BlockSpec((part, 1), lambda i: (i, 0))],
        out_specs=pl.BlockSpec((part, units), lambda i: (i, 0)),
    )
    return layer_output, step[None]


def local(
    activations,
    routed_experts,
    route_weights,
    live_counts,
    swap_partner,
    gate_proj,
    up_proj,
    down_proj,
    first_moment,
    second_moment,
):
    levels = swap_partner.shape[0].bit_length() - 1
    operands = (
        activations,
        routed_experts,
        route_weights,
        live_counts,
        gate_proj,
        up_proj,
        down_proj,
        first_moment,
        second_moment,
    )
    branches = [partial(work, shift_bit=bit) for bit in (levels - 2, levels - 1)]
    return lax.cond(swap_partner[0] == 1 << (levels - 1), branches[1], branches[0], operands)


def solution(mesh):
    in_specs = (
        P(("dp", "expert"), None),
        P(("dp", "expert"), None),
        P(("dp", "expert"), None),
        P("dp", "expert"),
        P(),
        P("expert", "dp", None),
        P("expert", "dp", None),
        P("expert", "dp", None),
        P("expert", "dp", None),
        P("expert", "dp"),
    )
    out_specs = (P(("dp", "expert"), None), P("expert", "dp", None))
    return jax.shard_map(local, mesh=mesh, in_specs=in_specs, out_specs=out_specs, check_vma=False)
```

```python
from functools import partial

import jax
import jax.numpy as jnp
from jax import lax
from jax.experimental import pallas as pl
from jax.experimental.pallas import tpu as pltpu
from jax.sharding import PartitionSpec as P

BF = jnp.bfloat16
F32 = jnp.float32
after = lax.optimization_barrier


def trade(block, axis, offset):
    count = lax.axis_size(axis)
    return lax.ppermute(block, axis, [(i, i ^ offset) for i in range(count)])


def by_offset(blocks, place):
    blocks = list(blocks)
    bit = 1
    while bit < len(blocks):
        on = (place & bit) == bit
        blocks = [jnp.where(on, blocks[i ^ bit], blocks[i]) for i in range(len(blocks))]
        bit *= 2
    return blocks


def rows_at(table, offset):
    parts = table.reshape(-1, 2, offset, table.shape[1])
    return jnp.concatenate([parts[:, 1:], parts[:, :1]], axis=1).reshape(table.shape)


def call(kernel, out_shape, *operands, **options):
    return pl.pallas_call(
        kernel,
        out_shape=out_shape,
        compiler_params=pltpu.CompilerParams(vmem_limit_bytes=16 << 20),
        **options,
    )(*operands)


def dot(a, b):
    return jnp.dot(a, b, preferred_element_type=F32)


def dot_columns(a, b):
    return lax.dot_general(a, b, (((1,), (1,)), ((), ())), preferred_element_type=F32)


def dot_rows(a, b):
    return lax.dot_general(a, b, (((0,), (0,)), ((), ())), preferred_element_type=F32)


def spread(table, capacity):
    experts, tokens = table.shape
    slots = experts * capacity
    chosen = table != 0
    earlier = lax.broadcasted_iota(jnp.int32, (tokens, tokens), 0)
    later = lax.broadcasted_iota(jnp.int32, (tokens, tokens), 1)
    rank = dot(jnp.where(chosen, 1.0, 0.0).astype(BF), jnp.where(earlier < later, 1.0, 0.0).astype(BF))
    rank = jnp.where(chosen, rank, -1.0).astype(BF)
    slot = lax.broadcasted_iota(jnp.int32, (slots, experts), 0)
    name = lax.broadcasted_iota(jnp.int32, (slots, experts), 1)
    owner = jnp.where(slot // capacity == name, 1.0, 0.0).astype(BF)
    place = (lax.broadcasted_iota(jnp.int32, (slots, tokens), 0) % capacity).astype(F32)
    return dot(owner, rank) == place, owner


def two_parts(value):
    high = value.astype(BF)
    return high, (value - high.astype(F32)).astype(BF)


def dispatch_kernel(place_ref, live_ref, ids_ref, weights_ref, act_ref, rows_ref, table_ref, *, capacity):
    experts, tokens = table_ref.shape
    lanes = max(experts, 128)
    name = lax.broadcasted_iota(jnp.int32, (tokens, lanes), 1)
    table = jnp.zeros((tokens, lanes), F32)
    for k in range(ids_ref.shape[1]):
        table = table + jnp.where(ids_ref[:, k : k + 1] == name, weights_ref[:, k : k + 1], 0.0)
    token = lax.broadcasted_iota(jnp.int32, (tokens, lanes), 0)
    table = jnp.where(token < live_ref[0, 0], table, -table)
    table = table.T[:experts]
    table_ref[...] = table
    chosen = jnp.where(spread(table, capacity)[0], 1.0, 0.0).astype(BF)
    block = act_ref.shape[1] // 4
    for i in range(4):
        source = pl.multiple_of((place_ref[0] ^ i) * block, block)
        rows_ref[:, i * block : (i + 1) * block] = dot(chosen, act_ref[:, pl.ds(source, block)]).astype(BF)


def gate_kernel(rows_ref, g0, g1, g2, g3, u0, u1, gate_ref, up_ref):
    block = g0.shape[0]
    columns = [rows_ref[:, i * block : (i + 1) * block] for i in range(4)]
    gate = sum(dot(c, w[...]) for c, w in zip(columns, (g0, g1, g2, g3)))
    gate_ref[...] = gate / (1.0 + jnp.exp(-gate))
    up_ref[...] = sum(dot(c, w[...]) for c, w in zip(columns, (u0, u1)))


def hidden_kernel(rows_ref, u2, u3, gate_ref, up_ref, hidden_ref):
    block = u2.shape[0]
    up = up_ref[...] + dot(rows_ref[:, 2 * block : 3 * block], u2[...])
    up = up + dot(rows_ref[:, 3 * block :], u3[...])
    hidden_ref[...] = (gate_ref[...] * up).astype(BF)


def moving_kernel(hidden_ref, second_ref, out_ref):
    rows, units = hidden_ref.shape
    block = second_ref.shape[1]
    out_ref[:rows] = hidden_ref[...]
    below = jnp.broadcast_to(second_ref[...].astype(F32), (16, block))
    below = jnp.concatenate([below, jnp.zeros((16, units - block), F32)], axis=1)
    out_ref[rows:] = below.astype(BF)


def produce_kernel(*refs):
    *hidden, down_ref, out_ref = refs
    block = down_ref.shape[0]
    for g, ref in enumerate(hidden):
        out_ref[:, g * block : (g + 1) * block] = dot_columns(ref[...], down_ref[...]).astype(BF)


def maps_kernel(tables_ref, placed_ref, back_ref, sent_ref, weight_ref, *, capacity):
    for g in range(tables_ref.shape[0]):
        table = tables_ref[g]
        chosen, owner = spread(table, capacity)
        for i, part in enumerate(two_parts(jnp.maximum(table, 0.0))):
            back_ref[g, i] = jnp.where(chosen, dot(owner, part), 0.0).T.astype(BF)
        table = placed_ref[g]
        chosen, owner = spread(table, capacity)
        sent_ref[g] = jnp.where(chosen, 1.0, 0.0).astype(BF)
        high, low = two_parts(jnp.abs(table))
        weight = dot(owner, high) + dot(owner, low)
        weight_ref[g] = jnp.sum(jnp.where(chosen, weight, 0.0), axis=1, keepdims=True)


def combine_kernel(rows_ref, back_ref, sent_ref, weight_ref, o0, o1, o2, o3, cot_ref):
    for g, out_ref in enumerate((o0, o1, o2, o3)):
        columns = slice(g * out_ref.shape[1], (g + 1) * out_ref.shape[1])
        rows = rows_ref[:, columns]
        out = (dot(back_ref[g, 0], rows) + dot(back_ref[g, 1], rows)).astype(BF)
        out_ref[...] = out
        cot_ref[:, columns] = (dot(sent_ref[g], out) * weight_ref[g]).astype(BF)


def step_kernel(cot_ref, h0, h1, h2, h3, second_ref, *refs):
    *firsts, out_ref = refs
    routed = cot_ref.shape[0]
    block = out_ref.shape[0]
    part = block // 2
    first = jnp.concatenate([f[...] for f in firsts], axis=0)
    for start in range(0, block, part):
        rows = slice(start, start + part)
        gradient = 0.0
        for g, hidden in enumerate((h0, h1, h2, h3)):
            columns = slice(g * block + start, g * block + start + part)
            gradient = gradient + dot_rows(cot_ref[:, columns], hidden[:routed])
        first_new = 0.9 * first[rows].astype(F32) + 0.1 * gradient
        mean = jnp.sum(gradient * gradient, axis=1, keepdims=True) * (1.0 / gradient.shape[1])
        second_new = 0.99 * second_ref[rows].astype(F32) + 0.01 * mean
        out_ref[rows] = (first_new / (jnp.sqrt(second_new) + 1e-08)).astype(BF)


def shape(*dims, dtype=BF):
    return jax.ShapeDtypeStruct(dims, dtype)


SCALARS = pl.BlockSpec(memory_space=pltpu.SMEM)
WHOLE = pl.BlockSpec(memory_space=pltpu.VMEM)


def work(operands, shift_bit):
    (
        activations,
        routed_experts,
        route_weights,
        live_counts,
        gate_proj,
        up_proj,
        down_proj,
        first_moment,
        second_moment,
    ) = operands
    offset = 1 << shift_bit
    experts = lax.axis_size("expert")
    place = lax.axis_index("dp")
    tokens, choices = routed_experts.shape
    routed = tokens * choices
    capacity = routed // experts
    width = activations.shape[1]
    block, units = gate_proj.shape[1:]

    def exchange(rows):
        cut = rows.reshape(experts, capacity, rows.shape[1])
        return lax.all_to_all(cut, "expert", split_axis=0, concat_axis=0, tiled=True).reshape(rows.shape)

    gate, up, down = gate_proj[0], up_proj[0], down_proj[0]
    gate2 = trade(gate, "dp", 2)
    up_late, gate2 = after((up, gate2))
    up2 = trade(up_late, "dp", 2)
    gate1, up1 = trade(gate, "dp", 1), trade(up, "dp", 1)

    outgoing, table = call(
        partial(dispatch_kernel, capacity=capacity),
        (shape(routed, width), shape(experts, tokens, dtype=F32)),
        jnp.stack([place]).astype(jnp.int32),
        live_counts,
        routed_experts,
        route_weights,
        activations,
        in_specs=[SCALARS, SCALARS, WHOLE, WHOLE, WHOLE],
    )
    shares = (0,0,4) if shift_bit == experts.bit_length() - 3 else (1,0,3)
    quarter = block // 4
    ends = [sum(shares[:i]) * quarter for i in range(4)]

    def moment(source, i):
        return trade(source[0, ends[i] : ends[i + 1]], "expert", offset) if shares[i] else None

    first_a = moment(first_moment, 0)
    if first_a is not None:
        outgoing, first_a = after((outgoing, first_a))
    arrived = exchange(outgoing)
    first_late, _ = after((first_moment, arrived))
    first_b = moment(first_late, 1)

    gate3 = trade(gate2, "dp", 1)
    gate_sum, up_sum = call(
        gate_kernel,
        (shape(routed, units, dtype=F32),) * 2,
        arrived,
        gate,
        gate1,
        gate2,
        gate3,
        up,
        up1,
        in_specs=[WHOLE] * 7,
    )
    up3 = trade(up2, "dp", 1)
    if first_b is not None:
        up_sum, first_b = after((up_sum, first_b))
    hidden = call(
        hidden_kernel,
        shape(routed, units),
        arrived,
        up2,
        up3,
        gate_sum,
        up_sum,
        in_specs=[WHOLE] * 5,
    )
    hidden2 = trade(hidden, "dp", 2)
    moving = call(moving_kernel, shape(routed + 16, units), hidden, second_moment)
    moved = trade(moving, "expert", offset)
    hidden1 = trade(hidden, "dp", 1)
    first_c = moment(first_late, 2)
    hidden2, first_c = after((hidden2, first_c))
    hidden3 = trade(hidden2, "dp", 1)
    made = call(produce_kernel, shape(routed, 4 * block), hidden, hidden1, hidden2, hidden3, down)
    back = exchange(made)

    table_late, moved = after((table, moved))
    table2 = trade(table_late, "dp", 2)
    table1, table3 = trade(jnp.stack([table, table2]), "dp", 1)
    tables = [table, table1, table2, table3]
    back_map, sent_map, sent_weight = call(
        partial(maps_kernel, capacity=capacity),
        (shape(4, 2, tokens, routed), shape(4, routed, tokens), shape(4, routed, 1, dtype=F32)),
        jnp.stack(tables),
        jnp.stack([rows_at(t, offset) for t in tables]),
    )
    moved, _ = after((moved, back))
    moved2 = trade(moved, "dp", 2)
    moved1 = trade(moved, "dp", 1)
    moved3 = trade(moved2, "dp", 1)

    out0, out1, out2, out3, cot = call(
        combine_kernel,
        [shape(tokens, block)] * 4 + [shape(routed, 4 * block)],
        back,
        back_map,
        sent_map,
        sent_weight,
    )
    cot = exchange(cot)

    mine = [out0, trade(out1, "dp", 1), trade(out2, "dp", 2), trade(out3, "dp", 3)]
    layer_output = jnp.concatenate(by_offset(mine, place), axis=1)

    second = moved[routed, :block].reshape(block, 1)
    step = call(
        step_kernel,
        shape(block, units),
        cot,
        moved,
        moved1,
        moved2,
        moved3,
        second,
        *[f for f in (first_a, first_b, first_c) if f is not None],
    )
    return layer_output, step[None]


def local(
    activations,
    routed_experts,
    route_weights,
    live_counts,
    swap_partner,
    gate_proj,
    up_proj,
    down_proj,
    first_moment,
    second_moment,
):
    levels = swap_partner.shape[0].bit_length() - 1
    operands = (
        activations,
        routed_experts,
        route_weights,
        live_counts,
        gate_proj,
        up_proj,
        down_proj,
        first_moment,
        second_moment,
    )
    branches = [partial(work, shift_bit=bit) for bit in (levels - 2, levels - 1)]
    return lax.cond(swap_partner[0] == 1 << (levels - 1), branches[1], branches[0], operands)


def solution(mesh):
    in_specs = (
        P(("dp", "expert"), None),
        P(("dp", "expert"), None),
        P(("dp", "expert"), None),
        P("dp", "expert"),
        P(),
        P("expert", "dp", None),
        P("expert", "dp", None),
        P("expert", "dp", None),
        P("expert", "dp", None),
        P("expert", "dp"),
    )
    out_specs = (P(("dp", "expert"), None), P("expert", "dp", None))
    return jax.shard_map(local, mesh=mesh, in_specs=in_specs, out_specs=out_specs, check_vma=False)
```

```python
from functools import partial

import jax
import jax.numpy as jnp
from jax import lax
from jax.experimental import pallas as pl
from jax.experimental.pallas import tpu as pltpu
from jax.sharding import PartitionSpec as P

BF = jnp.bfloat16
F32 = jnp.float32
after = lax.optimization_barrier


def trade(block, axis, offset):
    count = lax.axis_size(axis)
    return lax.ppermute(block, axis, [(i, i ^ offset) for i in range(count)])


def by_offset(blocks, place):
    blocks = list(blocks)
    bit = 1
    while bit < len(blocks):
        on = (place & bit) == bit
        blocks = [jnp.where(on, blocks[i ^ bit], blocks[i]) for i in range(len(blocks))]
        bit *= 2
    return blocks


def rows_at(table, offset):
    parts = table.reshape(-1, 2, offset, table.shape[1])
    return jnp.concatenate([parts[:, 1:], parts[:, :1]], axis=1).reshape(table.shape)


def call(kernel, out_shape, *operands, **options):
    return pl.pallas_call(
        kernel,
        out_shape=out_shape,
        compiler_params=pltpu.CompilerParams(vmem_limit_bytes=16 << 20),
        **options,
    )(*operands)


def dot(a, b):
    return jnp.dot(a, b, preferred_element_type=F32)


def dot_columns(a, b):
    return lax.dot_general(a, b, (((1,), (1,)), ((), ())), preferred_element_type=F32)


def dot_rows(a, b):
    return lax.dot_general(a, b, (((0,), (0,)), ((), ())), preferred_element_type=F32)


def spread(table, capacity):
    experts, tokens = table.shape
    slots = experts * capacity
    chosen = table != 0
    earlier = lax.broadcasted_iota(jnp.int32, (tokens, tokens), 0)
    later = lax.broadcasted_iota(jnp.int32, (tokens, tokens), 1)
    rank = dot(jnp.where(chosen, 1.0, 0.0).astype(BF), jnp.where(earlier < later, 1.0, 0.0).astype(BF))
    rank = jnp.where(chosen, rank, -1.0).astype(BF)
    slot = lax.broadcasted_iota(jnp.int32, (slots, experts), 0)
    name = lax.broadcasted_iota(jnp.int32, (slots, experts), 1)
    owner = jnp.where(slot // capacity == name, 1.0, 0.0).astype(BF)
    place = (lax.broadcasted_iota(jnp.int32, (slots, tokens), 0) % capacity).astype(F32)
    return dot(owner, rank) == place, owner


def two_parts(value):
    high = value.astype(BF)
    return high, (value - high.astype(F32)).astype(BF)


def dispatch_kernel(place_ref, live_ref, ids_ref, weights_ref, act_ref, rows_ref, table_ref, *, capacity):
    experts, tokens = table_ref.shape
    lanes = max(experts, 128)
    name = lax.broadcasted_iota(jnp.int32, (tokens, lanes), 1)
    table = jnp.zeros((tokens, lanes), F32)
    for k in range(ids_ref.shape[1]):
        table = table + jnp.where(ids_ref[:, k : k + 1] == name, weights_ref[:, k : k + 1], 0.0)
    token = lax.broadcasted_iota(jnp.int32, (tokens, lanes), 0)
    table = jnp.where(token < live_ref[0, 0], table, -table)
    table = table.T[:experts]
    table_ref[...] = table
    chosen = jnp.where(spread(table, capacity)[0], 1.0, 0.0).astype(BF)
    block = act_ref.shape[1] // 4
    for i in range(4):
        source = pl.multiple_of((place_ref[0] ^ i) * block, block)
        rows_ref[:, i * block : (i + 1) * block] = dot(chosen, act_ref[:, pl.ds(source, block)]).astype(BF)


def gate_kernel(rows_ref, g0, g1, g2, g3, u0, u1, gate_ref, up_ref):
    block = g0.shape[0]
    columns = [rows_ref[:, i * block : (i + 1) * block] for i in range(4)]
    gate = sum(dot(c, w[...]) for c, w in zip(columns, (g0, g1, g2, g3)))
    gate_ref[...] = gate / (1.0 + jnp.exp(-gate))
    up_ref[...] = sum(dot(c, w[...]) for c, w in zip(columns, (u0, u1)))


def hidden_kernel(rows_ref, u2, u3, gate_ref, up_ref, hidden_ref):
    block = u2.shape[0]
    up = up_ref[...] + dot(rows_ref[:, 2 * block : 3 * block], u2[...])
    up = up + dot(rows_ref[:, 3 * block :], u3[...])
    hidden_ref[...] = (gate_ref[...] * up).astype(BF)


def moving_kernel(hidden_ref, second_ref, out_ref):
    rows, units = hidden_ref.shape
    block = second_ref.shape[1]
    out_ref[:rows] = hidden_ref[...]
    below = jnp.broadcast_to(second_ref[...].astype(F32), (16, block))
    below = jnp.concatenate([below, jnp.zeros((16, units - block), F32)], axis=1)
    out_ref[rows:] = below.astype(BF)


def produce_kernel(*refs):
    *hidden, down_ref, out_ref = refs
    block = down_ref.shape[0]
    for g, ref in enumerate(hidden):
        out_ref[:, g * block : (g + 1) * block] = dot_columns(ref[...], down_ref[...]).astype(BF)


def maps_kernel(tables_ref, placed_ref, back_ref, sent_ref, weight_ref, *, capacity):
    for g in range(tables_ref.shape[0]):
        table = tables_ref[g]
        chosen, owner = spread(table, capacity)
        for i, part in enumerate(two_parts(jnp.maximum(table, 0.0))):
            back_ref[g, i] = jnp.where(chosen, dot(owner, part), 0.0).T.astype(BF)
        table = placed_ref[g]
        chosen, owner = spread(table, capacity)
        sent_ref[g] = jnp.where(chosen, 1.0, 0.0).astype(BF)
        ones = jnp.ones((weight_ref.shape[1], table.shape[1]), BF)
        weight = 0.0
        for part in two_parts(jnp.abs(table)):
            weight = weight + dot_columns(ones, jnp.where(chosen, dot(owner, part), 0.0).astype(BF))
        weight_ref[g] = weight


def combine_kernel(rows_ref, back_ref, sent_ref, weight_ref, o0, o1, o2, o3, cot_ref):
    for g, out_ref in enumerate((o0, o1, o2, o3)):
        columns = slice(g * out_ref.shape[1], (g + 1) * out_ref.shape[1])
        rows = rows_ref[:, columns]
        out = (dot(back_ref[g, 0], rows) + dot(back_ref[g, 1], rows)).astype(BF)
        out_ref[...] = out
        cot_ref[:, columns] = (dot(sent_ref[g], out) * weight_ref[g].T[:, :1]).astype(BF)


def step_kernel(cot_ref, h0, h1, h2, h3, second_ref, *refs):
    *firsts, out_ref = refs
    routed = cot_ref.shape[0]
    block = out_ref.shape[0]
    part = block // 2
    first = jnp.concatenate([f[...] for f in firsts], axis=0)
    second = jnp.broadcast_to(second_ref[...].astype(F32), (8, block)).T[:, :1]
    for start in range(0, block, part):
        rows = slice(start, start + part)
        gradient = 0.0
        for g, hidden in enumerate((h0, h1, h2, h3)):
            columns = slice(g * block + start, g * block + start + part)
            gradient = gradient + dot_rows(cot_ref[:, columns], hidden[:routed])
        first_new = 0.9 * first[rows].astype(F32) + 0.1 * gradient
        mean = jnp.sum(gradient * gradient, axis=1, keepdims=True) * (1.0 / gradient.shape[1])
        second_new = 0.99 * second[rows] + 0.01 * mean
        out_ref[rows] = (first_new / (jnp.sqrt(second_new) + 1e-08)).astype(BF)


def shape(*dims, dtype=BF):
    return jax.ShapeDtypeStruct(dims, dtype)


SCALARS = pl.BlockSpec(memory_space=pltpu.SMEM)
WHOLE = pl.BlockSpec(memory_space=pltpu.VMEM)


def work(operands, shift_bit):
    (
        activations,
        routed_experts,
        route_weights,
        live_counts,
        gate_proj,
        up_proj,
        down_proj,
        first_moment,
        second_moment,
    ) = operands
    offset = 1 << shift_bit
    experts = lax.axis_size("expert")
    place = lax.axis_index("dp")
    tokens, choices = routed_experts.shape
    routed = tokens * choices
    capacity = routed // experts
    width = activations.shape[1]
    block, units = gate_proj.shape[1:]

    def exchange(rows):
        cut = rows.reshape(experts, capacity, rows.shape[1])
        return lax.all_to_all(cut, "expert", split_axis=0, concat_axis=0, tiled=True).reshape(rows.shape)

    gate, up, down = gate_proj[0], up_proj[0], down_proj[0]
    gate2 = trade(gate, "dp", 2)
    up_late, gate2 = after((up, gate2))
    up2 = trade(up_late, "dp", 2)
    gate1, up1 = trade(gate, "dp", 1), trade(up, "dp", 1)

    outgoing, table = call(
        partial(dispatch_kernel, capacity=capacity),
        (shape(routed, width), shape(experts, tokens, dtype=F32)),
        jnp.stack([place]).astype(jnp.int32),
        live_counts,
        routed_experts,
        route_weights,
        activations,
        in_specs=[SCALARS, SCALARS, WHOLE, WHOLE, WHOLE],
    )
    shares = (0,0,4) if shift_bit == experts.bit_length() - 3 else (1,0,3)
    quarter = block // 4
    ends = [sum(shares[:i]) * quarter for i in range(4)]

    def moment(source, i):
        return trade(source[0, ends[i] : ends[i + 1]], "expert", offset) if shares[i] else None

    first_a = moment(first_moment, 0)
    if first_a is not None:
        outgoing, first_a = after((outgoing, first_a))
    arrived = exchange(outgoing)
    first_late, _ = after((first_moment, arrived))
    first_b = moment(first_late, 1)

    gate3 = trade(gate2, "dp", 1)
    gate_sum, up_sum = call(
        gate_kernel,
        (shape(routed, units, dtype=F32),) * 2,
        arrived,
        gate,
        gate1,
        gate2,
        gate3,
        up,
        up1,
        in_specs=[WHOLE] * 7,
    )
    up3 = trade(up2, "dp", 1)
    if first_b is not None:
        up_sum, first_b = after((up_sum, first_b))
    hidden = call(
        hidden_kernel,
        shape(routed, units),
        arrived,
        up2,
        up3,
        gate_sum,
        up_sum,
        in_specs=[WHOLE] * 5,
    )
    hidden2 = trade(hidden, "dp", 2)
    moving = call(moving_kernel, shape(routed + 16, units), hidden, second_moment)
    moved = trade(moving, "expert", offset)
    hidden1 = trade(hidden, "dp", 1)
    first_c = moment(first_late, 2)
    hidden2, first_c = after((hidden2, first_c))
    hidden3 = trade(hidden2, "dp", 1)
    made = call(produce_kernel, shape(routed, 4 * block), hidden, hidden1, hidden2, hidden3, down)
    back = exchange(made)

    table_late, moved = after((table, moved))
    table2 = trade(table_late, "dp", 2)
    table1, table3 = trade(jnp.stack([table, table2]), "dp", 1)
    tables = [table, table1, table2, table3]
    back_map, sent_map, sent_weight = call(
        partial(maps_kernel, capacity=capacity),
        (shape(4, 2, tokens, routed), shape(4, routed, tokens), shape(4, 8, routed, dtype=F32)),
        jnp.stack(tables),
        jnp.stack([rows_at(t, offset) for t in tables]),
    )
    moved, _ = after((moved, back))
    moved2 = trade(moved, "dp", 2)
    moved1 = trade(moved, "dp", 1)
    moved3 = trade(moved2, "dp", 1)

    out0, out1, out2, out3, cot = call(
        combine_kernel,
        [shape(tokens, block)] * 4 + [shape(routed, 4 * block)],
        back,
        back_map,
        sent_map,
        sent_weight,
    )
    cot = exchange(cot)

    mine = [out0, trade(out1, "dp", 1), trade(out2, "dp", 2), trade(out3, "dp", 3)]
    layer_output = jnp.concatenate(by_offset(mine, place), axis=1)

    second = moved[routed : routed + 1, :block]
    step = call(
        step_kernel,
        shape(block, units),
        cot,
        moved,
        moved1,
        moved2,
        moved3,
        second,
        *[f for f in (first_a, first_b, first_c) if f is not None],
    )
    return layer_output, step[None]


def local(
    activations,
    routed_experts,
    route_weights,
    live_counts,
    swap_partner,
    gate_proj,
    up_proj,
    down_proj,
    first_moment,
    second_moment,
):
    levels = swap_partner.shape[0].bit_length() - 1
    operands = (
        activations,
        routed_experts,
        route_weights,
        live_counts,
        gate_proj,
        up_proj,
        down_proj,
        first_moment,
        second_moment,
    )
    branches = [partial(work, shift_bit=bit) for bit in (levels - 2, levels - 1)]
    return lax.cond(swap_partner[0] == 1 << (levels - 1), branches[1], branches[0], operands)


def solution(mesh):
    in_specs = (
        P(("dp", "expert"), None),
        P(("dp", "expert"), None),
        P(("dp", "expert"), None),
        P("dp", "expert"),
        P(),
        P("expert", "dp", None),
        P("expert", "dp", None),
        P("expert", "dp", None),
        P("expert", "dp", None),
        P("expert", "dp"),
    )
    out_specs = (P(("dp", "expert"), None), P("expert", "dp", None))
    return jax.shard_map(local, mesh=mesh, in_specs=in_specs, out_specs=out_specs, check_vma=False)
```

```python
from functools import partial

import jax
import jax.numpy as jnp
from jax import lax
from jax.experimental import pallas as pl
from jax.experimental.pallas import tpu as pltpu
from jax.sharding import PartitionSpec as P

BF = jnp.bfloat16
F32 = jnp.float32
after = lax.optimization_barrier


def trade(block, axis, offset):
    count = lax.axis_size(axis)
    return lax.ppermute(block, axis, [(i, i ^ offset) for i in range(count)])


def by_offset(blocks, place):
    blocks = list(blocks)
    bit = 1
    while bit < len(blocks):
        on = (place & bit) == bit
        blocks = [jnp.where(on, blocks[i ^ bit], blocks[i]) for i in range(len(blocks))]
        bit *= 2
    return blocks


def rows_at(table, offset):
    parts = table.reshape(-1, 2, offset, table.shape[1])
    return jnp.concatenate([parts[:, 1:], parts[:, :1]], axis=1).reshape(table.shape)


def call(kernel, out_shape, *operands, **options):
    return pl.pallas_call(
        kernel,
        out_shape=out_shape,
        compiler_params=pltpu.CompilerParams(vmem_limit_bytes=16 << 20),
        **options,
    )(*operands)


def dot(a, b):
    return jnp.dot(a, b, preferred_element_type=F32)


def dot_columns(a, b):
    return lax.dot_general(a, b, (((1,), (1,)), ((), ())), preferred_element_type=F32)


def dot_rows(a, b):
    return lax.dot_general(a, b, (((0,), (0,)), ((), ())), preferred_element_type=F32)


def spread(table, capacity):
    experts, tokens = table.shape
    slots = experts * capacity
    chosen = table != 0
    earlier = lax.broadcasted_iota(jnp.int32, (tokens, tokens), 0)
    later = lax.broadcasted_iota(jnp.int32, (tokens, tokens), 1)
    rank = dot(jnp.where(chosen, 1.0, 0.0).astype(BF), jnp.where(earlier < later, 1.0, 0.0).astype(BF))
    rank = jnp.where(chosen, rank, -1.0).astype(BF)
    slot = lax.broadcasted_iota(jnp.int32, (slots, experts), 0)
    name = lax.broadcasted_iota(jnp.int32, (slots, experts), 1)
    owner = jnp.where(slot // capacity == name, 1.0, 0.0).astype(BF)
    place = (lax.broadcasted_iota(jnp.int32, (slots, tokens), 0) % capacity).astype(F32)
    return dot(owner, rank) == place, owner


def two_parts(value):
    high = value.astype(BF)
    return high, (value - high.astype(F32)).astype(BF)


def dispatch_kernel(place_ref, live_ref, ids_ref, weights_ref, act_ref, rows_ref, table_ref, *, capacity):
    experts, tokens = table_ref.shape
    lanes = max(experts, 128)
    name = lax.broadcasted_iota(jnp.int32, (tokens, lanes), 1)
    table = jnp.zeros((tokens, lanes), F32)
    for k in range(ids_ref.shape[1]):
        table = table + jnp.where(ids_ref[:, k : k + 1] == name, weights_ref[:, k : k + 1], 0.0)
    token = lax.broadcasted_iota(jnp.int32, (tokens, lanes), 0)
    table = jnp.where(token < live_ref[0, 0], table, -table)
    table = table.T[:experts]
    table_ref[...] = table
    chosen = jnp.where(spread(table, capacity)[0], 1.0, 0.0).astype(BF)
    block = act_ref.shape[1] // 4
    for i in range(4):
        source = pl.multiple_of((place_ref[0] ^ i) * block, block)
        rows_ref[:, i * block : (i + 1) * block] = dot(chosen, act_ref[:, pl.ds(source, block)]).astype(BF)


def gate_kernel(rows_ref, g0, g1, g2, g3, u0, u1, gate_ref, up_ref):
    block = g0.shape[0]
    columns = [rows_ref[:, i * block : (i + 1) * block] for i in range(4)]
    gate = sum(dot(c, w[...]) for c, w in zip(columns, (g0, g1, g2, g3)))
    gate_ref[...] = gate / (1.0 + jnp.exp(-gate))
    up_ref[...] = sum(dot(c, w[...]) for c, w in zip(columns, (u0, u1)))


def hidden_kernel(rows_ref, u2, u3, gate_ref, up_ref, hidden_ref):
    block = u2.shape[0]
    up = up_ref[...] + dot(rows_ref[:, 2 * block : 3 * block], u2[...])
    up = up + dot(rows_ref[:, 3 * block :], u3[...])
    hidden_ref[...] = (gate_ref[...] * up).astype(BF)


def moving_kernel(hidden_ref, second_ref, *refs):
    *first_ref, out_ref = refs
    rows, units = hidden_ref.shape
    block = second_ref.shape[1]
    out_ref[:rows] = hidden_ref[...]
    below = jnp.broadcast_to(second_ref[...].astype(F32), (16, block))
    below = jnp.concatenate([below, jnp.zeros((16, units - block), F32)], axis=1)
    out_ref[rows : rows + 16] = below.astype(BF)
    if first_ref:
        out_ref[rows + 16 :] = first_ref[0][0]


def produce_kernel(*refs):
    *hidden, down_ref, out_ref = refs
    block = down_ref.shape[0]
    for g, ref in enumerate(hidden):
        out_ref[:, g * block : (g + 1) * block] = dot_columns(ref[...], down_ref[...]).astype(BF)


def maps_kernel(tables_ref, placed_ref, back_ref, sent_ref, weight_ref, *, capacity):
    for g in range(tables_ref.shape[0]):
        table = tables_ref[g]
        chosen, owner = spread(table, capacity)
        for i, part in enumerate(two_parts(jnp.maximum(table, 0.0))):
            back_ref[g, i] = jnp.where(chosen, dot(owner, part), 0.0).T.astype(BF)
        table = placed_ref[g]
        chosen, owner = spread(table, capacity)
        sent_ref[g] = jnp.where(chosen, 1.0, 0.0).astype(BF)
        ones = jnp.ones((weight_ref.shape[1], table.shape[1]), BF)
        weight = 0.0
        for part in two_parts(jnp.abs(table)):
            weight = weight + dot_columns(ones, jnp.where(chosen, dot(owner, part), 0.0).astype(BF))
        weight_ref[g] = weight


def combine_kernel(rows_ref, back_ref, sent_ref, weight_ref, o0, o1, o2, o3, cot_ref):
    for g, out_ref in enumerate((o0, o1, o2, o3)):
        columns = slice(g * out_ref.shape[1], (g + 1) * out_ref.shape[1])
        rows = rows_ref[:, columns]
        out = (dot(back_ref[g, 0], rows) + dot(back_ref[g, 1], rows)).astype(BF)
        out_ref[...] = out
        cot_ref[:, columns] = (dot(sent_ref[g], out) * weight_ref[g].T[:, :1]).astype(BF)


def step_kernel(cot_ref, h0, h1, h2, h3, second_ref, *refs):
    *firsts, out_ref = refs
    routed = cot_ref.shape[0]
    block = out_ref.shape[0]
    part = block // 2
    first = jnp.concatenate([f[...] for f in firsts] + ([h0[routed + 16 :]] if h0.shape[0] > routed + 16 else []), axis=0)
    second = jnp.broadcast_to(second_ref[...].astype(F32), (8, block)).T[:, :1]
    for start in range(0, block, part):
        rows = slice(start, start + part)
        gradient = 0.0
        for g, hidden in enumerate((h0, h1, h2, h3)):
            columns = slice(g * block + start, g * block + start + part)
            gradient = gradient + dot_rows(cot_ref[:, columns], hidden[:routed])
        first_new = 0.9 * first[rows].astype(F32) + 0.1 * gradient
        mean = jnp.sum(gradient * gradient, axis=1, keepdims=True) * (1.0 / gradient.shape[1])
        second_new = 0.99 * second[rows] + 0.01 * mean
        out_ref[rows] = (first_new / (jnp.sqrt(second_new) + 1e-08)).astype(BF)


def shape(*dims, dtype=BF):
    return jax.ShapeDtypeStruct(dims, dtype)


SCALARS = pl.BlockSpec(memory_space=pltpu.SMEM)
WHOLE = pl.BlockSpec(memory_space=pltpu.VMEM)


def work(operands, shift_bit):
    (
        activations,
        routed_experts,
        route_weights,
        live_counts,
        gate_proj,
        up_proj,
        down_proj,
        first_moment,
        second_moment,
    ) = operands
    offset = 1 << shift_bit
    experts = lax.axis_size("expert")
    place = lax.axis_index("dp")
    tokens, choices = routed_experts.shape
    routed = tokens * choices
    capacity = routed // experts
    width = activations.shape[1]
    block, units = gate_proj.shape[1:]

    def exchange(rows):
        cut = rows.reshape(experts, capacity, rows.shape[1])
        return lax.all_to_all(cut, "expert", split_axis=0, concat_axis=0, tiled=True).reshape(rows.shape)

    gate, up, down = gate_proj[0], up_proj[0], down_proj[0]
    gate2 = trade(gate, "dp", 2)
    shares = (0, 6) if shift_bit == experts.bit_length() - 3 else (2, 6)
    unit = block // 8
    carried = block - sum(shares) * unit
    ends = [sum(shares[:i]) * unit for i in range(3)]
    early, middle = first_moment[0, : ends[1]], first_moment[0, ends[1] : ends[2]]
    if shares[0]:
        up_late, gate2 = after((up, gate2))
    else:
        up_late, gate2, middle = after((up, gate2, middle))
    up2 = trade(up_late, "dp", 2)
    gate1, up1 = trade(gate, "dp", 1), trade(up, "dp", 1)

    outgoing, table = call(
        partial(dispatch_kernel, capacity=capacity),
        (shape(routed, width), shape(experts, tokens, dtype=F32)),
        jnp.stack([place]).astype(jnp.int32),
        live_counts,
        routed_experts,
        route_weights,
        activations,
        in_specs=[SCALARS, SCALARS, WHOLE, WHOLE, WHOLE],
    )
    first_a = None
    if shares[0]:
        first_a = trade(early, "expert", offset)
        outgoing, first_a = after((outgoing, first_a))
    arrived = exchange(outgoing)
    middle, arrived = after((middle, arrived))

    gate3 = trade(gate2, "dp", 1)
    gate_sum, up_sum = call(
        gate_kernel,
        (shape(routed, units, dtype=F32),) * 2,
        arrived,
        gate,
        gate1,
        gate2,
        gate3,
        up,
        up1,
        in_specs=[WHOLE] * 7,
    )
    up3 = trade(up2, "dp", 1)
    hidden = call(
        hidden_kernel,
        shape(routed, units),
        arrived,
        up2,
        up3,
        gate_sum,
        up_sum,
        in_specs=[WHOLE] * 5,
    )
    hidden2 = trade(hidden, "dp", 2)
    moving = call(
        moving_kernel,
        shape(routed + 16 + carried, units),
        hidden,
        second_moment,
        *[first_moment] * (carried > 0),
        grid=(1,),
        in_specs=[
            pl.BlockSpec((routed, units), lambda i: (0, 0)),
            pl.BlockSpec((1, block), lambda i: (0, 0)),
        ]
        + [pl.BlockSpec((1, carried, units), lambda i: (0, block // carried - 1, 0))] * (carried > 0),
        out_specs=pl.BlockSpec((routed + 16 + carried, units), lambda i: (0, 0)),
    )
    moved = trade(moving, "expert", offset)
    hidden1 = trade(hidden, "dp", 1)
    first_c = trade(middle, "expert", offset)
    hidden2, first_c = after((hidden2, first_c))
    hidden3 = trade(hidden2, "dp", 1)
    made = call(produce_kernel, shape(routed, 4 * block), hidden, hidden1, hidden2, hidden3, down)
    back = exchange(made)

    table_late, moved = after((table, moved))
    table2 = trade(table_late, "dp", 2)
    table1, table3 = trade(jnp.stack([table, table2]), "dp", 1)
    tables = [table, table1, table2, table3]
    back_map, sent_map, sent_weight = call(
        partial(maps_kernel, capacity=capacity),
        (shape(4, 2, tokens, routed), shape(4, routed, tokens), shape(4, 8, routed, dtype=F32)),
        jnp.stack(tables),
        jnp.stack([rows_at(t, offset) for t in tables]),
    )
    moved, _ = after((moved, back))
    moved2 = trade(moved, "dp", 2)
    moved1 = trade(moved, "dp", 1)
    moved3 = trade(moved2, "dp", 1)

    out0, out1, out2, out3, cot = call(
        combine_kernel,
        [shape(tokens, block)] * 4 + [shape(routed, 4 * block)],
        back,
        back_map,
        sent_map,
        sent_weight,
    )
    cot = exchange(cot)

    mine = [out0, trade(out1, "dp", 1), trade(out2, "dp", 2), trade(out3, "dp", 3)]
    layer_output = jnp.concatenate(by_offset(mine, place), axis=1)

    second = moved[routed : routed + 1, :block]
    step = call(
        step_kernel,
        shape(block, units),
        cot,
        moved,
        moved1,
        moved2,
        moved3,
        second,
        *[f for f in (first_a, first_c) if f is not None],
    )
    return layer_output, step[None]


def local(
    activations,
    routed_experts,
    route_weights,
    live_counts,
    swap_partner,
    gate_proj,
    up_proj,
    down_proj,
    first_moment,
    second_moment,
):
    levels = swap_partner.shape[0].bit_length() - 1
    operands = (
        activations,
        routed_experts,
        route_weights,
        live_counts,
        gate_proj,
        up_proj,
        down_proj,
        first_moment,
        second_moment,
    )
    branches = [partial(work, shift_bit=bit) for bit in (levels - 2, levels - 1)]
    return lax.cond(swap_partner[0] == 1 << (levels - 1), branches[1], branches[0], operands)


def solution(mesh):
    in_specs = (
        P(("dp", "expert"), None),
        P(("dp", "expert"), None),
        P(("dp", "expert"), None),
        P("dp", "expert"),
        P(),
        P("expert", "dp", None),
        P("expert", "dp", None),
        P("expert", "dp", None),
        P("expert", "dp", None),
        P("expert", "dp"),
    )
    out_specs = (P(("dp", "expert"), None), P("expert", "dp", None))
    return jax.shard_map(local, mesh=mesh, in_specs=in_specs, out_specs=out_specs, check_vma=False)
```

```python
from functools import partial

import jax
import jax.numpy as jnp
from jax import lax
from jax.experimental import pallas as pl
from jax.experimental.pallas import tpu as pltpu
from jax.sharding import PartitionSpec as P

BF = jnp.bfloat16
F32 = jnp.float32
after = lax.optimization_barrier


def trade(block, axis, offset):
    count = lax.axis_size(axis)
    return lax.ppermute(block, axis, [(i, i ^ offset) for i in range(count)])


def by_offset(blocks, place):
    blocks = list(blocks)
    bit = 1
    while bit < len(blocks):
        on = (place & bit) == bit
        blocks = [jnp.where(on, blocks[i ^ bit], blocks[i]) for i in range(len(blocks))]
        bit *= 2
    return blocks


def rows_at(table, offset):
    parts = table.reshape(-1, 2, offset, table.shape[1])
    return jnp.concatenate([parts[:, 1:], parts[:, :1]], axis=1).reshape(table.shape)


def call(kernel, out_shape, *operands, **options):
    return pl.pallas_call(
        kernel,
        out_shape=out_shape,
        compiler_params=pltpu.CompilerParams(vmem_limit_bytes=16 << 20),
        **options,
    )(*operands)


def dot(a, b):
    return jnp.dot(a, b, preferred_element_type=F32)


def dot_columns(a, b):
    return lax.dot_general(a, b, (((1,), (1,)), ((), ())), preferred_element_type=F32)


def dot_rows(a, b):
    return lax.dot_general(a, b, (((0,), (0,)), ((), ())), preferred_element_type=F32)


def spread(table, capacity):
    experts, tokens = table.shape
    slots = experts * capacity
    chosen = table != 0
    earlier = lax.broadcasted_iota(jnp.int32, (tokens, tokens), 0)
    later = lax.broadcasted_iota(jnp.int32, (tokens, tokens), 1)
    rank = dot(jnp.where(chosen, 1.0, 0.0).astype(BF), jnp.where(earlier < later, 1.0, 0.0).astype(BF))
    rank = jnp.where(chosen, rank, -1.0).astype(BF)
    slot = lax.broadcasted_iota(jnp.int32, (slots, experts), 0)
    name = lax.broadcasted_iota(jnp.int32, (slots, experts), 1)
    owner = jnp.where(slot // capacity == name, 1.0, 0.0).astype(BF)
    place = (lax.broadcasted_iota(jnp.int32, (slots, tokens), 0) % capacity).astype(F32)
    return dot(owner, rank) == place, owner


def two_parts(value):
    high = value.astype(BF)
    return high, (value - high.astype(F32)).astype(BF)


def dispatch_kernel(place_ref, live_ref, ids_ref, weights_ref, act_ref, rows_ref, table_ref, *, capacity):
    experts, tokens = table_ref.shape
    lanes = max(experts, 128)
    name = lax.broadcasted_iota(jnp.int32, (tokens, lanes), 1)
    table = jnp.zeros((tokens, lanes), F32)
    for k in range(ids_ref.shape[1]):
        table = table + jnp.where(ids_ref[:, k : k + 1] == name, weights_ref[:, k : k + 1], 0.0)
    token = lax.broadcasted_iota(jnp.int32, (tokens, lanes), 0)
    table = jnp.where(token < live_ref[0, 0], table, -table)
    table = table.T[:experts]
    table_ref[...] = table
    chosen = jnp.where(spread(table, capacity)[0], 1.0, 0.0).astype(BF)
    block = act_ref.shape[1] // 4
    for i in range(4):
        source = pl.multiple_of((place_ref[0] ^ i) * block, block)
        rows_ref[:, i * block : (i + 1) * block] = dot(chosen, act_ref[:, pl.ds(source, block)]).astype(BF)


def gate_kernel(rows_ref, g0, g1, g2, g3, u0, u1, gate_ref, up_ref):
    block = g0.shape[0]
    columns = [rows_ref[:, i * block : (i + 1) * block] for i in range(4)]
    gate = sum(dot(c, w[...]) for c, w in zip(columns, (g0, g1, g2, g3)))
    gate_ref[...] = gate / (1.0 + jnp.exp(-gate))
    up_ref[...] = sum(dot(c, w[...]) for c, w in zip(columns, (u0, u1)))


def hidden_kernel(rows_ref, u2, u3, gate_ref, up_ref, hidden_ref):
    block = u2.shape[0]
    up = up_ref[...] + dot(rows_ref[:, 2 * block : 3 * block], u2[...])
    up = up + dot(rows_ref[:, 3 * block :], u3[...])
    hidden_ref[...] = (gate_ref[...] * up).astype(BF)


def moving_kernel(hidden_ref, second_ref, *refs):
    *first_ref, out_ref = refs
    rows, units = hidden_ref.shape
    block = second_ref.shape[1]
    out_ref[:rows] = hidden_ref[...]
    below = jnp.broadcast_to(second_ref[...].astype(F32), (16, block))
    below = jnp.concatenate([below, jnp.zeros((16, units - block), F32)], axis=1)
    out_ref[rows : rows + 16] = below.astype(BF)
    if first_ref:
        out_ref[rows + 16 :] = first_ref[0][0]


def produce_kernel(*refs):
    *hidden, down_ref, out_ref = refs
    block = down_ref.shape[0]
    for g, ref in enumerate(hidden):
        out_ref[:, g * block : (g + 1) * block] = dot_columns(ref[...], down_ref[...]).astype(BF)


def maps_kernel(tables_ref, placed_ref, back_ref, sent_ref, weight_ref, *, capacity):
    for g in range(tables_ref.shape[0]):
        table = tables_ref[g]
        chosen, owner = spread(table, capacity)
        for i, part in enumerate(two_parts(jnp.maximum(table, 0.0))):
            back_ref[g, i] = jnp.where(chosen, dot(owner, part), 0.0).T.astype(BF)
        table = placed_ref[g]
        chosen, owner = spread(table, capacity)
        sent_ref[g] = jnp.where(chosen, 1.0, 0.0).astype(BF)
        ones = jnp.ones((weight_ref.shape[1], table.shape[1]), BF)
        weight = 0.0
        for part in two_parts(jnp.abs(table)):
            weight = weight + dot_columns(ones, jnp.where(chosen, dot(owner, part), 0.0).astype(BF))
        weight_ref[g] = weight


def combine_kernel(rows_ref, back_ref, sent_ref, weight_ref, o0, o1, o2, o3, cot_ref):
    for g, out_ref in enumerate((o0, o1, o2, o3)):
        columns = slice(g * out_ref.shape[1], (g + 1) * out_ref.shape[1])
        rows = rows_ref[:, columns]
        out = (dot(back_ref[g, 0], rows) + dot(back_ref[g, 1], rows)).astype(BF)
        out_ref[...] = out
        cot_ref[:, columns] = (dot(sent_ref[g], out) * weight_ref[g].T[:, :1]).astype(BF)


def step_kernel(cot_ref, h0, h1, h2, h3, second_ref, *refs):
    *firsts, out_ref = refs
    routed = cot_ref.shape[0]
    block = out_ref.shape[0]
    part = block // 2
    first = jnp.concatenate([f[...] for f in firsts] + ([h0[routed + 16 :]] if h0.shape[0] > routed + 16 else []), axis=0)
    second = jnp.broadcast_to(second_ref[...].astype(F32), (8, block)).T[:, :1]
    for start in range(0, block, part):
        rows = slice(start, start + part)
        gradient = 0.0
        for g, hidden in enumerate((h0, h1, h2, h3)):
            columns = slice(g * block + start, g * block + start + part)
            gradient = gradient + dot_rows(cot_ref[:, columns], hidden[:routed])
        first_new = 0.9 * first[rows].astype(F32) + 0.1 * gradient
        mean = jnp.sum(gradient * gradient, axis=1, keepdims=True) * (1.0 / gradient.shape[1])
        second_new = 0.99 * second[rows] + 0.01 * mean
        out_ref[rows] = (first_new / (jnp.sqrt(second_new) + 1e-08)).astype(BF)


def shape(*dims, dtype=BF):
    return jax.ShapeDtypeStruct(dims, dtype)


SCALARS = pl.BlockSpec(memory_space=pltpu.SMEM)
WHOLE = pl.BlockSpec(memory_space=pltpu.VMEM)


def work(operands, shift_bit):
    (
        activations,
        routed_experts,
        route_weights,
        live_counts,
        gate_proj,
        up_proj,
        down_proj,
        first_moment,
        second_moment,
    ) = operands
    offset = 1 << shift_bit
    experts = lax.axis_size("expert")
    place = lax.axis_index("dp")
    tokens, choices = routed_experts.shape
    routed = tokens * choices
    capacity = routed // experts
    width = activations.shape[1]
    block, units = gate_proj.shape[1:]

    def exchange(rows):
        cut = rows.reshape(experts, capacity, rows.shape[1])
        return lax.all_to_all(cut, "expert", split_axis=0, concat_axis=0, tiled=True).reshape(rows.shape)

    gate, up, down = gate_proj[0], up_proj[0], down_proj[0]
    gate2 = trade(gate, "dp", 2)
    shares = (0, 6) if shift_bit == experts.bit_length() - 3 else (2, 6)
    unit = block // 8
    carried = block - sum(shares) * unit
    ends = [sum(shares[:i]) * unit for i in range(3)]
    early, middle = first_moment[0, : ends[1]], first_moment[0, ends[1] : ends[2]]
    if shares[0]:
        up_late, gate2 = after((up, gate2))
    else:
        up_late, gate2, middle = after((up, gate2, middle))
    up2 = trade(up_late, "dp", 2)
    gate1, up1 = trade(gate, "dp", 1), trade(up, "dp", 1)

    outgoing, table = call(
        partial(dispatch_kernel, capacity=capacity),
        (shape(routed, width), shape(experts, tokens, dtype=F32)),
        jnp.stack([place]).astype(jnp.int32),
        live_counts,
        routed_experts,
        route_weights,
        activations,
        in_specs=[SCALARS, SCALARS, WHOLE, WHOLE, WHOLE],
    )
    first_a = None
    if shares[0]:
        first_a = trade(early, "expert", offset)
        outgoing, first_a = after((outgoing, first_a))
    arrived = exchange(outgoing)
    middle, arrived = after((middle, arrived))

    gate3 = trade(gate2, "dp", 1)
    gate_sum, up_sum = call(
        gate_kernel,
        (shape(routed, units, dtype=F32),) * 2,
        arrived,
        gate,
        gate1,
        gate2,
        gate3,
        up,
        up1,
        in_specs=[WHOLE] * 7,
    )
    up3 = trade(up2, "dp", 1)
    hidden = call(
        hidden_kernel,
        shape(routed, units),
        arrived,
        up2,
        up3,
        gate_sum,
        up_sum,
        in_specs=[WHOLE] * 5,
    )
    hidden2 = trade(hidden, "dp", 2)
    moving = call(
        moving_kernel,
        shape(routed + 16 + carried, units),
        hidden,
        second_moment,
        *[first_moment] * (carried > 0),
        grid=(1,),
        in_specs=[
            pl.BlockSpec((routed, units), lambda i: (0, 0)),
            pl.BlockSpec((1, block), lambda i: (0, 0)),
        ]
        + [pl.BlockSpec((1, carried, units), lambda i: (0, block // carried - 1, 0))] * (carried > 0),
        out_specs=pl.BlockSpec((routed + 16 + carried, units), lambda i: (0, 0)),
    )
    moved = trade(moving, "expert", offset)
    hidden1 = trade(hidden, "dp", 1)
    first_c = trade(middle, "expert", offset)
    hidden2, first_c = after((hidden2, first_c))
    hidden3 = trade(hidden2, "dp", 1)
    made = call(produce_kernel, shape(routed, 4 * block), hidden, hidden1, hidden2, hidden3, down)
    back = exchange(made)

    table_late, moved = after((table, moved))
    table2 = trade(table_late, "dp", 2)
    table1, table3 = trade(jnp.stack([table, table2]), "dp", 1)
    tables = [table, table1, table2, table3]
    back_map, sent_map, sent_weight = call(
        partial(maps_kernel, capacity=capacity),
        (shape(4, 2, tokens, routed), shape(4, routed, tokens), shape(4, 8, routed, dtype=F32)),
        jnp.stack(tables),
        jnp.stack([rows_at(t, offset) for t in tables]),
    )
    moved, _ = after((moved, back))
    moved_rows = moved[:routed]
    moved2 = trade(moved_rows, "dp", 2)
    moved1 = trade(moved_rows, "dp", 1)
    moved3 = trade(moved2, "dp", 1)

    out0, out1, out2, out3, cot = call(
        combine_kernel,
        [shape(tokens, block)] * 4 + [shape(routed, 4 * block)],
        back,
        back_map,
        sent_map,
        sent_weight,
    )
    cot = exchange(cot)

    mine = [out0, trade(out1, "dp", 1), trade(out2, "dp", 2), trade(out3, "dp", 3)]
    layer_output = jnp.concatenate(by_offset(mine, place), axis=1)

    second = moved[routed : routed + 1, :block]
    step = call(
        step_kernel,
        shape(block, units),
        cot,
        moved,
        moved1,
        moved2,
        moved3,
        second,
        *[f for f in (first_a, first_c) if f is not None],
    )
    return layer_output, step[None]


def local(
    activations,
    routed_experts,
    route_weights,
    live_counts,
    swap_partner,
    gate_proj,
    up_proj,
    down_proj,
    first_moment,
    second_moment,
):
    levels = swap_partner.shape[0].bit_length() - 1
    operands = (
        activations,
        routed_experts,
        route_weights,
        live_counts,
        gate_proj,
        up_proj,
        down_proj,
        first_moment,
        second_moment,
    )
    branches = [partial(work, shift_bit=bit) for bit in (levels - 2, levels - 1)]
    return lax.cond(swap_partner[0] == 1 << (levels - 1), branches[1], branches[0], operands)


def solution(mesh):
    in_specs = (
        P(("dp", "expert"), None),
        P(("dp", "expert"), None),
        P(("dp", "expert"), None),
        P("dp", "expert"),
        P(),
        P("expert", "dp", None),
        P("expert", "dp", None),
        P("expert", "dp", None),
        P("expert", "dp", None),
        P("expert", "dp"),
    )
    out_specs = (P(("dp", "expert"), None), P("expert", "dp", None))
    return jax.shard_map(local, mesh=mesh, in_specs=in_specs, out_specs=out_specs, check_vma=False)
```
